128 devices in a mesh: seq: 8 (over x, y_hi), tensor: 16 (over y_lo, z, core).
Axes of the slice: x: 4, y: 4 (y_hi: 2, y_lo: 2; y = y_hi * 2 + y_lo), z: 4, core: 2. Of those that a mesh axis runs over, the one named last changes fastest.
Arguments:
- tokens: bfloat16 [4096, 4096], P(('seq', 'tensor')), may hold values from -6 to 6
- cotangent: bfloat16 [4096, 4096], P(('seq', 'tensor')), may hold values from -6 to 6
- task_ids: int32 [16], replicated, may hold values from 0 to 63
- gate_matrix: bfloat16 [4096, 12288], P(None, 'tensor'), may hold values from -0.09375 to 0.09375
- up_matrix: bfloat16 [4096, 12288], P(None, 'tensor'), may hold values from -0.09375 to 0.09375
- down_weight: bfloat16 [12288, 4096], P('tensor'), may hold values from -0.0546875 to 0.0546875
- shrink_factors: bfloat16 [64, 32, 4096], P(None, None, 'tensor'), may hold values from -0.09375 to 0.09375
- expand_factors: bfloat16 [64, 32, 12288], P(None, None, 'tensor'), may hold values from -1.5 to 1.5
Outputs:
- mixed: bfloat16 [4096, 4096], P(('seq', 'tensor'))
- grad_tokens: bfloat16 [4096, 4096], P(('seq', 'tensor'))
- grad_shrink: float32 [64, 32, 4096], P('seq', None, 'tensor')
- expand_gradient: float32 [64, 32, 12288], P('seq', None, 'tensor')
The draws below stay inside these ranges and needn't reach their ends.
All inputs are finite; a program needn't handle non-finite values.
Results may differ from the reference program's by a relative error of at most 0.009.
Values may be sent and summed in bfloat16 or wider, within the bound.
A program may use at most 128 MiB of HBM per device.

```python
import math
import jax
import jax.numpy as jnp
import numpy as np
from jax import lax

MODEL_WIDTH = 4096
HIDDEN_UNITS = 12288
ADAPTER_RANK = 16
TASKS = 64
BLOCK = 256
TOKENS = 4096
NBLK = 16


def place_ends(drawn, own_key, smallest, top_value):
    shape = drawn.shape
    index_at = [jax.random.randint(jax.random.fold_in(own_key, axis), (), 0, shape[axis]) for axis in range(len(shape))]
    drawn = drawn.at[tuple(index_at)].set(smallest)
    longest = shape.index(max(shape))
    index_at[longest] = (index_at[longest] + 1) % shape[longest]
    return drawn.at[tuple(index_at)].set(top_value)


def shard_levels(key, dims, shards, smallest, largest):
    factor_of = 1.0
    for axis_at, blocks in shards:
        steps = jax.random.uniform(jax.random.fold_in(jax.random.fold_in(key, 6), axis_at), (blocks,), jnp.float32, smallest / len(shards), largest / len(shards))
        factor_of = factor_of * jnp.repeat(jnp.exp(steps), dims[axis_at] // blocks).reshape((-1,) + (1,) * (len(dims) - 1 - axis_at))
    return factor_of


def rank_bounds(count, skew):
    portions = [(1 << 20) // math.isqrt(grade ** skew) + 1 for grade in range(1, count + 1)]
    spread = 1 + sum(portions) // (1 << 30)
    return np.cumsum(np.array([max(1, weight // spread) for weight in portions]))


def ranked_ids(stream_key, dims, count, lean):
    table = rank_bounds(count, lean)
    ticket = jax.random.randint(jax.random.fold_in(stream_key, 1), dims, 0, int(table[count - 1]))
    standing = jnp.searchsorted(jnp.asarray(table, jnp.int32), ticket, side="right")
    return jax.random.permutation(jax.random.fold_in(stream_key, 2), count)[standing].astype(jnp.int32)


def scatter_about(stream_key, dims, scale, limit, split=(), kind=jnp.bfloat16):
    entries = jax.random.normal(stream_key, dims, jnp.float32) * scale
    if len(split) > 0:
        entries = shard_levels(stream_key, dims, split, -0.22, 0.18) * entries
    return jnp.clip(entries, min=-limit, max=limit).astype(kind)


def setup_inputs(seed: int = 0) -> dict:
    keys = jax.random.split(jax.random.key(seed), 9)
    return {
        "tokens": scatter_about(keys[0], (TOKENS, MODEL_WIDTH), 1.0, 6.0, ((0, 128),)),
        "cotangent": scatter_about(keys[1], (TOKENS, MODEL_WIDTH), 1.0, 6.0, ((0, 128),)),
        "task_ids": place_ends(ranked_ids(keys[2], (NBLK,), TASKS, 2), jax.random.fold_in(keys[2], 3), 0, TASKS - 1).astype(jnp.int32),
        "gate_matrix": scatter_about(keys[3], (MODEL_WIDTH, HIDDEN_UNITS), MODEL_WIDTH ** -0.5, 0.09375, ((1, 16),)),
        "up_matrix": scatter_about(keys[4], (MODEL_WIDTH, HIDDEN_UNITS), MODEL_WIDTH ** -0.5, 0.09375, ((1, 16),)),
        "down_weight": scatter_about(keys[5], (HIDDEN_UNITS, MODEL_WIDTH), HIDDEN_UNITS ** -0.5, 0.0546875, ((0, 16),)),
        "shrink_factors": scatter_about(keys[6], (TASKS, 2 * ADAPTER_RANK, MODEL_WIDTH), MODEL_WIDTH ** -0.5, 0.09375, ((2, 16),)),
        "expand_factors": scatter_about(keys[7], (TASKS, 2 * ADAPTER_RANK, HIDDEN_UNITS), ADAPTER_RANK ** -0.5, 1.5, ((2, 16),)),
    }


def reference(tokens, cotangent, task_ids, gate_matrix, up_matrix, down_weight, shrink_factors, expand_factors):
    block_count = task_ids.shape[0]
    shrink_selected = shrink_factors[task_ids].astype(jnp.float32)
    expand_selected = expand_factors[task_ids].astype(jnp.float32)
    token_blocks = tokens.reshape(block_count, BLOCK, MODEL_WIDTH).astype(jnp.float32)
    shrunk_low = lax.optimization_barrier(jnp.einsum('nbd,nrd->nbr', token_blocks, shrink_selected).astype(jnp.bfloat16))
    reduced_input = shrunk_low.astype(jnp.float32)
    adapter_gate_term = jnp.einsum('yos,ysm->yom', reduced_input[..., :ADAPTER_RANK], expand_selected[:, :ADAPTER_RANK]).reshape(-1, HIDDEN_UNITS)
    adapter_up_term = jnp.einsum('yos,ysm->yom', reduced_input[..., ADAPTER_RANK:], expand_selected[:, ADAPTER_RANK:]).reshape(-1, HIDDEN_UNITS)
    gate_preactivation = jnp.dot(tokens, gate_matrix, preferred_element_type=jnp.float32) + adapter_gate_term
    up_preactivation = jnp.dot(tokens, up_matrix, preferred_element_type=jnp.float32) + adapter_up_term
    sigmoid_gate = jax.nn.sigmoid(gate_preactivation)
    silu_gate = gate_preactivation * sigmoid_gate
    hidden = (silu_gate * up_preactivation).astype(jnp.bfloat16)
    mixed = jnp.dot(hidden, down_weight, preferred_element_type=jnp.float32).astype(jnp.bfloat16)
    grad_hidden = jnp.dot(cotangent, down_weight.T, preferred_element_type=jnp.float32)
    grad_gate = lax.optimization_barrier((grad_hidden * up_preactivation * sigmoid_gate * (1.0 + gate_preactivation * (1.0 - sigmoid_gate))).astype(jnp.bfloat16))
    up_gradient = lax.optimization_barrier((grad_hidden * silu_gate).astype(jnp.bfloat16))
    gate_blocks = grad_gate.reshape(block_count, BLOCK, HIDDEN_UNITS).astype(jnp.float32)
    up_blocks = up_gradient.reshape(block_count, BLOCK, HIDDEN_UNITS).astype(jnp.float32)
    reduced_gradient = jnp.concatenate([
        jnp.einsum('nbf,nrf->nbr', gate_blocks, expand_selected[:, :ADAPTER_RANK]),
        jnp.einsum('nbf,nrf->nbr', up_blocks, expand_selected[:, ADAPTER_RANK:])], axis=2)
    reduced_gradient = lax.optimization_barrier(reduced_gradient.astype(jnp.bfloat16)).astype(jnp.float32)
    adapter_input_rows = jnp.einsum('jap,jpc->jac', reduced_gradient, shrink_selected).reshape(-1, MODEL_WIDTH)
    grad_tokens = (jnp.dot(grad_gate, gate_matrix.T, preferred_element_type=jnp.float32)
                   + jnp.dot(up_gradient, up_matrix.T, preferred_element_type=jnp.float32) + adapter_input_rows).astype(jnp.bfloat16)
    expand_per_block = jnp.concatenate([
        jnp.einsum('nbr,nbf->nrf', reduced_input[..., :ADAPTER_RANK], gate_blocks),
        jnp.einsum('nbr,nbf->nrf', reduced_input[..., ADAPTER_RANK:], up_blocks)], axis=1)
    block_shrink = jnp.einsum('nbr,nbd->nrd', reduced_gradient, token_blocks)
    task_indicator = (jnp.arange(TASKS, dtype=jnp.int32)[:, None] == task_ids[None, :]).astype(jnp.float32)
    grad_shrink = jnp.einsum('tn,nrd->trd', task_indicator, block_shrink, precision=lax.Precision.HIGHEST)
    expand_gradient = jnp.einsum('us,svk->uvk', task_indicator, expand_per_block, precision=lax.Precision.HIGHEST)
    return mixed, grad_tokens, grad_shrink, expand_gradient
```

```python
import jax
import jax.numpy as jnp
from jax import lax
from jax.experimental import pallas as pl
from jax.experimental.pallas import tpu as pltpu
from jax.sharding import PartitionSpec as P

BLOCK = 256
MESH = pl.DeviceIdType.MESH
BF = jnp.bfloat16
F32 = jnp.float32
WIN = 256
CHUNKS = 4
NT = (((1,), (1,)), ((), ()))
TN = (((0,), (0,)), ((), ()))


def kernel(
    ids, tok, cot, gate_h, up_h, down_h, shr_h, exp_h,
    mixed_o, grad_o, gsh_o, gex_o,
    gate, up, down, shr, expd, xb, cb, sf, shk, egu, pre_g, pre_u, hid, gg, gu,
    part, dr, yr, hb, fb, gs_half, gs_recv, gs_all, gs_tot, adapt, ex_send, ex_recv, sh_send, sh_nb, sh_recv,
    ge, gsh, loc, ss, rs,
):
    width = tok.shape[1]
    hidden = gate_h.shape[1]
    cw = width // CHUNKS
    seq = lax.axis_index("seq")
    ten = lax.axis_index("tensor")
    x, yh = lax.div(seq, 2), lax.rem(seq, 2)
    yl, z, c = lax.div(ten, 8), lax.rem(lax.div(ten, 2), 4), lax.rem(ten, 2)
    y = yh * 2 + yl
    other = 1 - c

    def mod4(v):
        return lax.rem(v, 4)

    zp, zm, zz = mod4(z + 1), mod4(z + 3), mod4(z + 2)
    yp, ym, yo = mod4(y + 1), mod4(y + 3), mod4(y + 2)
    yd, ys = mod4(y + 1 + 2 * c), mod4(y + 3 + 2 * c)
    xp, xm, xo = mod4(x + 1), mod4(x + 3), mod4(x + 2)

    def dev(dx, dy, dz, dc):
        return {"seq": dx * 2 + lax.div(dy, 2), "tensor": lax.rem(dy, 2) * 8 + dz * 2 + dc}

    d_zp, d_zm = dev(x, y, zp, c), dev(x, y, zm, c)
    d_core = dev(x, y, z, other)
    d_yd, d_ys = dev(x, yd, z, c), dev(x, ys, z, c)
    d_ydo = dev(x, yd, z, other)
    d_yo = dev(x, yo, z, c)
    d_xp, d_xm = dev(xp, y, z, c), dev(xm, y, z, c)
    column = [dev(x, y, mod4(z + k // 2), lax.rem(c + k % 2, 2)) for k in range(1, 8)]

    sent = []

    def send(src, dst, i, to):
        copy = pltpu.make_async_remote_copy(
            src_ref=src, dst_ref=dst, send_sem=ss.at[i], recv_sem=rs.at[i],
            device_id=to, device_id_type=MESH,
        )
        copy.start()
        sent.append(copy)

    def arrived(dst, i):
        pltpu.make_async_remote_copy(
            src_ref=dst, dst_ref=dst, send_sem=ss.at[i], recv_sem=rs.at[i],
            device_id=d_core, device_id_type=MESH,
        ).wait_recv()

    local = []

    def fetch(src, dst):
        copy = pltpu.make_async_copy(src, dst, loc.at[len(local)])
        copy.start()
        local.append(copy)
        return copy

    mid = pl.ds(WIN, width)
    f_shr = fetch(shr_h, shr)
    f_tok = fetch(tok, xb.at[c, z, :, mid])
    f_cot = fetch(cot, cb.at[c, z])
    f_gate = fetch(gate_h, gate)
    f_up = fetch(up_h, up)
    f_exp = fetch(exp_h, expd)
    f_down = fetch(down_h, down)

    barrier = pltpu.get_barrier_semaphore()
    greet = column + [d_yd, d_ys, d_ydo, d_yo, d_xp, d_xm]
    for to in greet:
        pl.semaphore_signal(barrier, inc=1, device_id=to, device_id_type=MESH)
    pl.semaphore_wait(barrier, len(greet))

    block = x * 4 + y
    f_shr.wait()
    f_tok.wait()
    xb[c, z, :, 0:WIN] = shr[ids[block]]
    xb[c, z, :, WIN + width : 2 * WIN + width] = shr[ids[x * 4 + yd]]

    order = [z, zm, zp, zz]
    all_x, lo_x, hi_x = pl.ds(0, width + 2 * WIN), pl.ds(0, width // 2 + WIN), pl.ds(width // 2 + WIN, width // 2 + WIN)
    own_x, nb_x = pl.ds(0, width + WIN), pl.ds(WIN, width + WIN)
    all_c, lo_c, hi_c = pl.ds(0, width), pl.ds(0, width // 2), pl.ds(width // 2, width // 2)

    class Gather:
        def __init__(self, buf, base, full, lo, hi, own, nb):
            self.buf, self.base, self.full, self.lo, self.hi, self.own, self.nb = buf, base, full, lo, hi, own, nb

        def at(self, q, zi, cols):
            return self.buf.at[q, zi, :, cols]

        def ring(self):
            ref = self.at(c, z, self.full)
            send(ref, ref, self.base, d_zp)
            send(ref, ref, self.base + 1, d_zm)

        def to_y(self, k):
            send(self.at(c, order[k], self.nb), self.at(2 + c, order[k], self.nb), self.base + 4 + k, d_yd)

        def to_core(self, k):
            ref = self.at(c, order[k], self.own)
            send(ref, ref, self.base + 8 + k, d_core)

        def ring_up(self):
            arrived(self.at(c, zm, self.full), self.base)
            ref = self.at(c, zm, self.lo)
            send(ref, ref, self.base + 2, d_zp)

        def ring_down(self):
            arrived(self.at(c, zp, self.full), self.base + 1)
            ref = self.at(c, zp, self.hi)
            send(ref, ref, self.base + 3, d_zm)

        def far(self):
            arrived(self.at(c, zz, self.lo), self.base + 2)
            arrived(self.at(c, zz, self.hi), self.base + 3)

        def y_to_core(self, k):
            ref = self.at(2 + c, order[k], self.nb)
            arrived(ref, self.base + 4 + k)
            send(ref, ref, self.base + 12 + k, d_core)

        def own_core(self):
            for k in range(4):
                arrived(self.at(other, order[k], self.own), self.base + 8 + k)

        def nb_core(self):
            for k in range(4):
                arrived(self.at(2 + other, order[k], self.nb), self.base + 12 + k)

    gx = Gather(xb, 0, all_x, lo_x, hi_x, own_x, nb_x)
    gc = Gather(cb, 16, all_c, lo_c, hi_c, all_c, all_c)

    gx.ring()
    gx.to_y(0)
    gx.to_core(0)
    gx.ring_up()
    gx.to_y(1)
    gx.to_core(1)
    gx.ring_down()
    gx.to_y(2)
    gx.to_core(2)
    f_cot.wait()
    gc.ring()
    gc.to_core(0)
    gx.far()
    gx.to_y(3)
    gx.to_core(3)
    gc.to_y(0)

    f_exp.wait()
    rank2 = exp_h.shape[1]
    low = lax.broadcasted_iota(jnp.int32, (rank2, hidden), 0) < rank2 // 2
    for k, yy in enumerate((y, ym, yp)):
        chosen = expd[ids[x * 4 + yy]]
        egu[k, 0] = jnp.where(low, chosen.astype(F32), 0.0).astype(BF)
        egu[k, 1] = jnp.where(low, 0.0, chosen.astype(F32)).astype(BF)

    f_gate.wait()
    f_up.wait()
    gx.own_core()

    def main_products(half):
        @pl.loop(0, hidden // 256)
        def _(n):
            cols = pl.ds(pl.multiple_of(n * 256, 256), 256)
            rows = xb[2 * half : 2 * half + 2, :, :, WIN : WIN + width].reshape(256, width)
            pre_g[half, :, cols] = jnp.dot(rows, gate[:, cols], preferred_element_type=F32)
            pre_u[half, :, cols] = jnp.dot(rows, up[:, cols], preferred_element_type=F32)

    main_products(0)
    for k in range(4):
        gx.y_to_core(k)
    gc.ring_up()
    gc.to_y(1)
    gc.to_core(1)
    gc.ring_down()
    gc.to_y(2)
    gc.to_core(2)
    gx.nb_core()

    for k in range(2):
        for zi in range(4):
            w_own = yl * 8 + zi * 2 + k
            w_nb = (1 - yl) * 8 + zi * 2 + k
            sf[:, pl.ds(pl.multiple_of(w_own * WIN, WIN), WIN)] = xb[k, zi, :, 0:WIN]
            sf[:, pl.ds(pl.multiple_of(w_nb * WIN, WIN), WIN)] = xb[2 + k, zi, :, WIN + width : 2 * WIN + width]
    shrunk = lax.dot_general(
        xb[0:2, :, :, WIN : WIN + width].reshape(256, width), sf[...], NT, preferred_element_type=F32
    ).astype(BF)
    shk[0, :, 0:rank2] = shrunk[0:128]
    shk[1, :, 0:rank2] = shrunk[128:256]
    S_SHK = 32
    send(shk.at[c], shk.at[2 + c], S_SHK, d_yd)
    send(shk.at[c], shk.at[2 + c], S_SHK + 1, d_ydo)

    main_products(1)
    gc.far()
    gc.to_y(3)
    gc.to_core(3)
    arrived(shk.at[2 + c], S_SHK)
    arrived(shk.at[2 + other], S_SHK + 1)

    def activations(q, k):
        half, r0 = q // 2, (q % 2) * 128

        @pl.loop(0, hidden // 256)
        def _(n):
            cols = pl.ds(pl.multiple_of(n * 256, 256), 256)
            s = shk[q, :, 0:rank2]
            g = pre_g[half, r0 : r0 + 128, cols] + jnp.dot(s, egu[k, 0, :, cols], preferred_element_type=F32)
            u = pre_u[half, r0 : r0 + 128, cols] + jnp.dot(s, egu[k, 1, :, cols], preferred_element_type=F32)
            sg = jax.nn.sigmoid(g)
            silu = g * sg
            hid[half, r0 : r0 + 128, cols] = (silu * u).astype(BF)
            pre_g[half, r0 : r0 + 128, cols] = u * sg * (1.0 + g * (1.0 - sg))
            pre_u[half, r0 : r0 + 128, cols] = silu

    activations(0, 0)
    activations(1, 0)
    activations(2, 1)
    activations(3, 2)
    f_down.wait()

    S_RED = 34

    class Reduce:
        def __init__(self, p, product):
            self.p, self.product = p, product

        def sem(self, what, j):
            return S_RED + (self.p * 6 + what) * CHUNKS + j

        def cols(self, j):
            return pl.ds(j * cw, cw)

        def partial(self, half, j):
            p, cols = self.p, self.cols(j)
            part[p, half, :, :, :, cols] = self.product(half, j).astype(BF).reshape(2, 4, 32, cw)
            send(part.at[p, half, other, :, :, cols], dr.at[p, half, :, :, cols], self.sem(half, j), d_core)

        def to_y(self, j):
            p, cols = self.p, self.cols(j)
            arrived(dr.at[p, 1, :, :, cols], self.sem(1, j))
            part[p, 1, c, :, :, cols] = (
                part[p, 1, c, :, :, cols].astype(F32) + dr[p, 1, :, :, cols].astype(F32)
            ).astype(BF)
            send(part.at[p, 1, c, :, :, cols], yr.at[p, :, :, cols], self.sem(2, j), d_ys)

        def to_far(self, j):
            p, cols = self.p, self.cols(j)
            arrived(dr.at[p, 0, :, :, cols], self.sem(0, j))
            arrived(yr.at[p, :, :, cols], self.sem(2, j))
            part[p, 0, c, :, :, cols] = (
                part[p, 0, c, :, :, cols].astype(F32)
                + dr[p, 0, :, :, cols].astype(F32)
                + yr[p, :, :, cols].astype(F32)
            ).astype(BF)
            if j % 2 == 0:
                send(part.at[p, 0, c, zz, :, cols], hb.at[p, :, cols], self.sem(3, j), d_zp)
                send(part.at[p, 0, c, zm, :, cols], fb.at[p, 1, :, cols], self.sem(5, j), d_zm)
            else:
                send(part.at[p, 0, c, zz, :, cols], hb.at[p, :, cols], self.sem(3, j), d_zm)
                send(part.at[p, 0, c, zp, :, cols], fb.at[p, 0, :, cols], self.sem(4, j), d_zp)

        def to_near(self, j):
            p, cols = self.p, self.cols(j)
            owner = zp if j % 2 == 0 else zm
            arrived(hb.at[p, :, cols], self.sem(3, j))
            part[p, 0, c, owner, :, cols] = (
                part[p, 0, c, owner, :, cols].astype(F32) + hb[p, :, cols].astype(F32)
            ).astype(BF)
            if j % 2 == 0:
                send(part.at[p, 0, c, zp, :, cols], fb.at[p, 0, :, cols], self.sem(4, j), d_zp)
            else:
                send(part.at[p, 0, c, zm, :, cols], fb.at[p, 1, :, cols], self.sem(5, j), d_zm)

        def result(self, j):
            p, cols = self.p, self.cols(j)
            arrived(fb.at[p, 0, :, cols], self.sem(4, j))
            arrived(fb.at[p, 1, :, cols], self.sem(5, j))
            return (
                part[p, 0, c, z, :, cols].astype(F32)
                + fb[p, 0, :, cols].astype(F32)
                + fb[p, 1, :, cols].astype(F32)
            )

    def mixed_product(half, j):
        return jnp.dot(hid[half], down[:, j * cw : (j + 1) * cw], preferred_element_type=F32)

    def grad_product(half, j):
        rows = slice(j * cw, (j + 1) * cw)
        return lax.dot_general(gg[half], gate[rows, :], NT, preferred_element_type=F32) + lax.dot_general(
            gu[half], up[rows, :], NT, preferred_element_type=F32
        )

    rm = Reduce(0, mixed_product)
    rg = Reduce(1, grad_product)

    for j in range(CHUNKS):
        rm.partial(1, j)
    for j in range(CHUNKS):
        rm.partial(0, j)
        rm.to_y(j)

    def gradients(half):
        @pl.loop(0, hidden // 256)
        def _(n):
            cols = pl.ds(pl.multiple_of(n * 256, 256), 256)
            rows = cb[2 * half : 2 * half + 2].reshape(256, width)
            gh = lax.dot_general(rows, down[cols, :], NT, preferred_element_type=F32)
            gg[half, :, cols] = (gh * pre_g[half, :, cols]).astype(BF)
            gu[half, :, cols] = (gh * pre_u[half, :, cols]).astype(BF)

    gc.own_core()
    gradients(0)
    for k in range(4):
        gc.y_to_core(k)
    gc.nb_core()
    gradients(1)

    S_GS, S_EX, S_SH, S_RING = S_RED + 12 * CHUNKS, S_RED + 12 * CHUNKS + 9, S_RED + 12 * CHUNKS + 10, S_RED + 12 * CHUNKS + 12
    quarters = ((0, 0, 256, 0), (1, 0, 128, 1), (1, 128, 256, 2))

    def shrunk_gradient(half, r0, r1, k):
        return lax.dot_general(egu[k, 0], gg[half, r0:r1, :], NT, preferred_element_type=F32) + lax.dot_general(
            egu[k, 1], gu[half, r0:r1, :], NT, preferred_element_type=F32
        )

    d_yp, d_ym = dev(x, yp, z, c), dev(x, ym, z, c)
    gs_half[0] = shrunk_gradient(*quarters[1])
    gs_half[1] = shrunk_gradient(*quarters[2])
    send(gs_half.at[0], gs_recv.at[0], S_GS, d_ym)
    send(gs_half.at[1], gs_recv.at[1], S_GS + 1, d_yp)

    def expand_part(s, half, r0, r1):
        a = lax.dot_general(s, gg[half, r0:r1, :], TN, preferred_element_type=F32)
        b = lax.dot_general(s, gu[half, r0:r1, :], TN, preferred_element_type=F32)
        return jnp.where(low, a, b).astype(BF)

    ex_send[0] = expand_part(shk[0:2, :, 0:rank2].reshape(256, rank2), 0, 0, 256)
    ex_send[1] = expand_part(shk[2, :, 0:rank2], 1, 0, 128)
    ex_send[2] = expand_part(shk[3, :, 0:rank2], 1, 128, 256)
    send(ex_send, ex_recv, S_EX, d_yo)

    for j in range(CHUNKS):
        rg.partial(1, j)

    here = z * 2 + c
    own_gs = shrunk_gradient(*quarters[0])
    arrived(gs_recv.at[0], S_GS)
    arrived(gs_recv.at[1], S_GS + 1)
    gs_all[here, 0] = own_gs[:, 0:128] + gs_recv[0]
    gs_all[here, 1] = own_gs[:, 128:256] + gs_recv[1]
    for k in range(1, 8):
        send(gs_all.at[here], gs_all.at[here], S_GS + 1 + k, column[k - 1])

    for j in range(CHUNKS):
        rg.partial(0, j)
        rg.to_y(j)

    arrived(ex_recv, S_EX)
    ge[x, y] = ex_send[0]
    ge[x, yo] = ex_recv[0]
    ge[x, ym] = (ex_send[1].astype(F32) + ex_recv[2].astype(F32)).astype(BF)
    ge[x, yp] = (ex_send[2].astype(F32) + ex_recv[1].astype(F32)).astype(BF)
    send(ge.at[x], ge.at[x], S_RING, d_xp)
    send(ge.at[x], ge.at[x], S_RING + 1, d_xm)

    for k in range(1, 8):
        source = mod4(z + 4 - k // 2) * 2 + lax.rem(c + k % 2, 2)
        arrived(gs_all.at[source], S_GS + 1 + k)
    for k in range(2):
        total = gs_all[0, k]
        for i in range(1, 8):
            total = total + gs_all[i, k]
        gs_tot[k] = total.astype(BF)

    def window_gradient(w):
        cols = pl.ds(pl.multiple_of(WIN + w * WIN, WIN), WIN)
        return (
            jnp.dot(gs_tot[0], xb[0, :, :, cols].reshape(128, WIN), preferred_element_type=F32)
            + jnp.dot(gs_tot[1], xb[1, :, :, cols].reshape(128, WIN), preferred_element_type=F32)
        ).astype(BF)

    sh_nb[...] = window_gradient((1 - yl) * 8 + here)
    send(sh_nb, sh_send.at[1], S_SH, d_yd)
    sh_send[0] = window_gradient(yl * 8 + here)

    pick = (
        lax.broadcasted_iota(jnp.int32, (32, 128), 1) == z * 32 + lax.broadcasted_iota(jnp.int32, (32, 128), 0)
    ).astype(F32).astype(BF)
    own_rows = lax.dot_general(pick, gs_tot[c], NT, preferred_element_type=F32).astype(BF)
    adapt[...] = jnp.dot(own_rows, sf[...], preferred_element_type=F32)

    for j in range(CHUNKS):
        rm.to_far(j)
    for j in range(CHUNKS):
        rm.to_near(j)

    arrived(sh_send.at[1], S_SH)
    send(sh_send, sh_recv, S_SH + 1, d_yo)

    arrived(ge.at[xm], S_RING)
    send(ge.at[xm, 0:2], ge.at[xm, 0:2], S_RING + 2, d_xp)
    arrived(ge.at[xp], S_RING + 1)
    send(ge.at[xp, 2:4], ge.at[xp, 2:4], S_RING + 3, d_xm)

    for j in range(CHUNKS):
        mixed_o[:, j * cw : (j + 1) * cw] = rm.result(j).astype(BF)

    arrived(sh_recv, S_SH + 1)
    gsh[x, y] = sh_send[0]
    gsh[x, ys] = sh_send[1]
    gsh[x, yo] = sh_recv[0]
    gsh[x, yd] = sh_recv[1]
    send(gsh.at[x], gsh.at[x], S_RING + 4, d_xp)
    send(gsh.at[x], gsh.at[x], S_RING + 5, d_xm)

    for j in range(CHUNKS):
        rg.to_far(j)

    arrived(gsh.at[xm], S_RING + 4)
    send(gsh.at[xm, 0:2], gsh.at[xm, 0:2], S_RING + 6, d_xp)
    arrived(gsh.at[xp], S_RING + 5)
    send(gsh.at[xp, 2:4], gsh.at[xp, 2:4], S_RING + 7, d_xm)

    for j in range(CHUNKS):
        rg.to_near(j)

    own_tasks = gex_o.shape[0]

    def by_task(src, out):
        @pl.loop(0, out.shape[2] // 128)
        def _(n):
            cols = pl.ds(pl.multiple_of(n * 128, 128), 128)
            sums = [jnp.zeros((rank2, 128), F32) for _ in range(own_tasks)]
            for k in range(16):
                value = src[k // 4, k % 4, :, cols].astype(F32)
                for i in range(own_tasks):
                    weight = jnp.where(ids[k] == seq * own_tasks + i, 1.0, 0.0)
                    sums[i] = sums[i] + value * weight
            for i in range(own_tasks):
                out[i, :, cols] = sums[i]

    arrived(ge.at[xo, 0:2], S_RING + 2)
    arrived(ge.at[xo, 2:4], S_RING + 3)
    by_task(ge, gex_o)
    arrived(gsh.at[xo, 0:2], S_RING + 6)
    arrived(gsh.at[xo, 2:4], S_RING + 7)
    by_task(gsh, gsh_o)

    for j in range(CHUNKS):
        cols = slice(j * cw, (j + 1) * cw)
        grad_o[:, cols] = (rg.result(j) + adapt[:, cols]).astype(BF)

    for copy in sent:
        copy.wait_send()


def on_device(tokens, cotangent, task_ids, gate_matrix, up_matrix, down_weight, shrink_factors, expand_factors):
    rows, width = tokens.shape
    hidden = gate_matrix.shape[1]
    tasks, rank2, window = shrink_factors.shape
    own_tasks = tasks // 8
    vmem = pl.BlockSpec(memory_space=pltpu.VMEM)
    hbm = pl.BlockSpec(memory_space=pl.ANY)
    copies = 34 + 12 * CHUNKS + 20
    return pl.pallas_call(
        kernel,
        out_shape=(
            jax.ShapeDtypeStruct((rows, width), BF),
            jax.ShapeDtypeStruct((rows, width), BF),
            jax.ShapeDtypeStruct((own_tasks, rank2, window), F32),
            jax.ShapeDtypeStruct((own_tasks, rank2, hidden), F32),
        ),
        in_specs=[pl.BlockSpec(memory_space=pltpu.SMEM)] + [hbm] * 7,
        out_specs=(vmem, vmem, vmem, vmem),
        scratch_shapes=[
            pltpu.VMEM((width, hidden), BF),
            pltpu.VMEM((width, hidden), BF),
            pltpu.VMEM((hidden, width), BF),
            pltpu.VMEM((tasks, rank2, window), BF),
            pltpu.VMEM((tasks, rank2, hidden), BF),
            pltpu.VMEM((4, 4, rows, width + 2 * window), BF),
            pltpu.VMEM((4, 4, rows, width), BF),
            pltpu.VMEM((rank2, width), BF),
            pltpu.VMEM((4, 128, 128), BF),
            pltpu.VMEM((3, 2, rank2, hidden), BF),
            pltpu.VMEM((2, 256, hidden), F32),
            pltpu.VMEM((2, 256, hidden), F32),
            pltpu.VMEM((2, 256, hidden), BF),
            pltpu.VMEM((2, 256, hidden), BF),
            pltpu.VMEM((2, 256, hidden), BF),
            pltpu.VMEM((2, 2, 2, 4, rows, width), BF),
            pltpu.VMEM((2, 2, 4, rows, width), BF),
            pltpu.VMEM((2, 4, rows, width), BF),
            pltpu.VMEM((2, rows, width), BF),
            pltpu.VMEM((2, 2, rows, width), BF),
            pltpu.VMEM((2, rank2, 128), F32),
            pltpu.VMEM((2, rank2, 128), F32),
            pltpu.VMEM((8, 2, rank2, 128), F32),
            pltpu.VMEM((2, rank2, 128), BF),
            pltpu.VMEM((rows, width), F32),
            pltpu.VMEM((3, rank2, hidden), BF),
            pltpu.VMEM((3, rank2, hidden), BF),
            pltpu.VMEM((2, rank2, window), BF),
            pltpu.VMEM((rank2, window), BF),
            pltpu.VMEM((2, rank2, window), BF),
            pltpu.VMEM((4, 4, rank2, hidden), BF),
            pltpu.VMEM((4, 4, rank2, window), BF),
            pltpu.SemaphoreType.DMA((7,)),
            pltpu.SemaphoreType.DMA((copies,)),
            pltpu.SemaphoreType.DMA((copies,)),
        ],
        compiler_params=pltpu.CompilerParams(
            collective_id=0, has_side_effects=True, vmem_limit_bytes=64 * 1024 * 1024 - 256 * 1024
        ),
        cost_estimate=pl.CostEstimate(
            flops=12 * 512 * width * hidden, bytes_accessed=6 * width * hidden, transcendentals=512 * hidden
        ),
    )(task_ids, tokens, cotangent, gate_matrix, up_matrix, down_weight, shrink_factors, expand_factors)


def solution(mesh):
    placed = (
        P(("seq", "tensor"), None),
        P(("seq", "tensor"), None),
        P(),
        P(None, "tensor"),
        P(None, "tensor"),
        P("tensor", None),
        P(None, None, "tensor"),
        P(None, None, "tensor"),
    )
    return jax.shard_map(
        on_device,
        mesh=mesh,
        in_specs=placed,
        out_specs=(
            P(("seq", "tensor"), None),
            P(("seq", "tensor"), None),
            P("seq", None, "tensor"),
            P("seq", None, "tensor"),
        ),
        check_vma=False,
    )
```
